32 devices in a mesh: parts: 2 (over y), tm: 4 (over x, core), span: 4 (over z).
Axes of the slice: x: 2, y: 2, z: 4, core: 2. Of those that a mesh axis runs over, the one named last changes fastest.
Arguments:
- start_state: float32 [2, 512, 1024], P(None, ('parts', 'span')), parts along dimension 1, may hold values from -4 to 4
- stiff_class: int32 [2048], P('parts'), parts along dimension 0, may hold values from 0 to 5
- class_stiffness: float32 [6], replicated, may hold values from 0.5 to 2
- axle_rows: int32 [64, 8], P(('parts', 'tm')), parts along dimension 0, may hold values from 0 to 255
- axle_cols: int32 [64, 8], P(('parts', 'tm')), parts along dimension 0, may hold values from 0 to 1023
- axle_class: int32 [64, 8], P(('parts', 'tm')), parts along dimension 0, may hold values from 0 to 4
- load_table: float32 [5], replicated, may hold values from 2 to 20
Outputs:
- end_states: float32 [4, 2, 512, 1024], P('tm', None, ('parts', 'span')), parts along dimension 2
The draws below stay inside these ranges and needn't reach their ends.
There are 2 independent parts, one for each index of `parts`. The reference program is written for one: setup_inputs(seed, part) draws one part's arguments, and reference() takes and returns one part's arrays. A program takes and returns all parts, laid end to end along the dimension named above; an argument that names none is the same for every part. Nothing has to cross between parts.
All inputs are finite; a program needn't handle non-finite values.
Results may differ from the reference program's by a relative error of at most 0.00027.
Values sent between devices are 32-bit elements; how exact they have to be, the bound alone decides.
A program may use at most 128 MiB of HBM per device.

```python
import math
import jax
import jax.numpy as jnp

W = 1024
FSTEPS = 8
AXLES = 8
NCLS = 6
NLOAD = 5
SLICES = 4
L = 256
LC = 64
WC = 256
STEPS = 32


def touch_ends(values, rng, smallest, largest):
    place = [jax.random.randint(jax.random.fold_in(rng, axis), (), 0, length) for axis, length in enumerate(values.shape)]
    longest = values.shape.index(max(values.shape))
    beside = place[:longest] + [(place[longest] + 1) % values.shape[longest]] + place[longest + 1:]
    return values.at[tuple(place)].set(smallest).at[tuple(beside)].set(largest)


def block_levels(key, extent, split, least, high):
    factor_of = 1.0
    for axis_at, shards_of in split:
        steps = jax.random.uniform(jax.random.fold_in(jax.random.fold_in(key, 6), axis_at), (shards_of,), jnp.float32, least / len(split), high / len(split))
        factor_of = factor_of * jnp.repeat(jnp.exp(steps), extent[axis_at] // shards_of).reshape((-1,) + (1,) * (len(extent) - 1 - axis_at))
    return factor_of


def noise(stream_key, dims, scale, most, shards=(), dtype=jnp.bfloat16):
    factor_of = block_levels(stream_key, dims, shards, -0.22, 0.18) if shards else 1.0
    values = jax.random.normal(stream_key, dims, jnp.float32) * scale * factor_of
    return jnp.minimum(jnp.maximum(values, -most), most).astype(dtype)


def setup_inputs(seed: int = 0, part: int = 0) -> dict:
    streams_of = jax.random.split(jax.random.key(seed), 8)
    part_keys = jax.random.split(jax.random.fold_in(streams_of[7], part), 8)
    start_state = noise(part_keys[0], (2, L, W), 0.5, 4.0, ((1, 4),), jnp.float32)
    stiff_class = touch_ends(jax.random.randint(part_keys[1], (W,), 0, NCLS), jax.random.fold_in(part_keys[1], 1), 0, NCLS - 1).astype(jnp.int32)
    class_stiffness = jnp.clip(jnp.exp(jax.random.uniform(streams_of[2], (NCLS,), jnp.float32, math.log(0.5), math.log(2.0))), 0.5, 2.0)
    axle_rows = touch_ends(jax.random.randint(part_keys[3], (STEPS, AXLES), 0, L), jax.random.fold_in(part_keys[3], 1), 0, L - 1).astype(jnp.int32)
    axle_cols = touch_ends(jax.random.randint(part_keys[4], (STEPS, AXLES), 0, W), jax.random.fold_in(part_keys[4], 1), 0, W - 1).astype(jnp.int32)
    axle_class = touch_ends(jax.random.randint(part_keys[5], (STEPS, AXLES), 0, NLOAD), jax.random.fold_in(part_keys[5], 1), 0, NLOAD - 1).astype(jnp.int32)
    load_table = jnp.clip(jnp.exp(jax.random.uniform(streams_of[6], (NLOAD,), jnp.float32, math.log(2.0), math.log(20.0))), 2.0, 20.0)
    return dict(start_state=start_state, stiff_class=stiff_class, class_stiffness=class_stiffness, axle_rows=axle_rows, axle_cols=axle_cols, axle_class=axle_class, load_table=load_table)


TIME_STEP = 0.2
DAMPING = 0.05
TWIST = 0.5
CROSS_STIFF = 1.0
COARSE_SPACING = 256.0


def stiffness_term(padded, column_stiff):
    widened = jnp.pad(padded, ((0, 0), (2, 2)))
    along_rows = widened[2:] - 2.0 * widened[1:-1] + widened[:-2]
    along_four = along_rows[2:] - 2.0 * along_rows[1:-1] + along_rows[:-2]
    across = widened[:, 2:] - 2.0 * widened[:, 1:-1] + widened[:, :-2]
    across_four = across[:, 2:] - 2.0 * across[:, 1:-1] + across[:, :-2]
    mixed_term = across[2:] - 2.0 * across[1:-1] + across[:-2]
    return column_stiff * along_four[:, 2:-2] + (2.0 * TWIST) * mixed_term[1:-1, 1:-1] + CROSS_STIFF * across_four[2:-2]


def advance(padded, deflect, velocity, column_stiff, loading, spacing, time_step):
    velocity = (1.0 - time_step * DAMPING) * velocity + time_step * (loading - stiffness_term(padded, column_stiff) / spacing)
    return deflect + time_step * velocity, velocity


def restrict(fine_field):
    leading = fine_field.shape[:-2]
    row_count = fine_field.shape[-2]
    col_count = fine_field.shape[-1]
    return jnp.mean(fine_field.reshape(leading + (row_count // 4, 4, col_count // 4, 4)), axis=(-3, -1))


def prolong(coarse):
    return jnp.repeat(jnp.repeat(coarse, 4, axis=-2), 4, axis=-1)


def reference(start_state, stiff_class, class_stiffness, axle_rows, axle_cols, axle_class, load_table):
    column_stiff = class_stiffness[stiff_class]
    coarse_stiff = jnp.mean(column_stiff.reshape(WC, 4), axis=-1)
    weights = load_table[axle_class]

    def fine_load(moment):
        return jnp.zeros((L, W), jnp.float32).at[axle_rows[moment], axle_cols[moment]].add(weights[moment])

    coarse_loads = []
    for slice_number in range(SLICES):
        total = jnp.zeros((LC, WC), jnp.float32)
        for substep in range(FSTEPS):
            total = total + restrict(fine_load(slice_number * FSTEPS + substep))
        coarse_loads.append(total / FSTEPS)

    def coarse_step(fields, slice_number):
        deflect, velocity = advance(jnp.pad(fields[0], ((2, 2), (0, 0))), fields[0], fields[1], coarse_stiff,
                                    coarse_loads[slice_number], COARSE_SPACING, TIME_STEP * FSTEPS)
        return jnp.stack([deflect, velocity])

    def fine_sweep(fields, slice_number):
        deflect, velocity = fields[0], fields[1]
        for substep in range(FSTEPS):
            loading = fine_load(slice_number * FSTEPS + substep)
            deflect, velocity = advance(jnp.pad(deflect, ((2, 2), (0, 0))), deflect, velocity, column_stiff,
                                        loading, 1.0, TIME_STEP)
        return jnp.stack([deflect, velocity])

    anchor = restrict(start_state)
    first_chain = [anchor]
    for slice_number in range(SLICES - 1):
        first_chain.append(coarse_step(first_chain[-1], slice_number))
    first_starts = [start_state] + [prolong(first_chain[k]) for k in range(1, SLICES)]
    first_sweeps = [fine_sweep(first_starts[k], k) for k in range(SLICES)]

    second_chain = [anchor]
    for slice_number in range(SLICES - 1):
        old_value = coarse_step(first_chain[slice_number], slice_number)
        second_chain.append(coarse_step(second_chain[-1], slice_number)
                            + (restrict(first_sweeps[slice_number]) - old_value))
    second_starts = [start_state] + [first_sweeps[k - 1] + prolong(second_chain[k] - restrict(first_sweeps[k - 1]))
                                     for k in range(1, SLICES)]
    second_sweeps = [fine_sweep(second_starts[k], k) for k in range(SLICES)]

    ends = []
    current = anchor
    for slice_number in range(SLICES):
        old_value = coarse_step(second_chain[slice_number], slice_number)
        following = coarse_step(current, slice_number) + (restrict(second_sweeps[slice_number]) - old_value)
        ends.append(second_sweeps[slice_number] + prolong(following - restrict(second_sweeps[slice_number])))
        current = following
    return jnp.stack(ends)
```

```python
import functools
import jax
import jax.numpy as jnp
from jax import lax
from jax.experimental import pallas as pl
from jax.experimental.pallas import tpu as pltpu
from jax.sharding import PartitionSpec as P

TIME_STEP = 0.2
DAMPING = 0.05
TWIST = 0.5
CROSS_STIFF = 1.0
COARSE_SPACING = 256.0
MESH = pl.DeviceIdType.MESH
PAD = 8
FAR = 32
NEAR = 16


def hot_split(value):
    high = value.astype(jnp.bfloat16)
    rest = value - high.astype(jnp.float32)
    mid = rest.astype(jnp.bfloat16)
    low = (rest - mid.astype(jnp.float32)).astype(jnp.bfloat16)
    return high, mid, low


def split_dot(value, ones):
    return sum(jnp.dot(term, ones, preferred_element_type=jnp.float32) for term in hot_split(value))


def first_pass(read, rows, chunks, stiff):
    lane = lax.broadcasted_iota(jnp.int32, (8, 128), 1)
    first, last = lane == 0, lane == 127
    zero = jnp.zeros((8, 128), jnp.float32)

    def neighbours(cells, before, after):
        up = [pltpu.roll(cell, 1, 1) for cell in cells]
        down = [pltpu.roll(cell, 127, 1) for cell in cells]
        left = [jnp.where(first, up[c - 1] if c else before, up[c]) for c in range(chunks)]
        right = [
            jnp.where(last, down[c + 1] if c < chunks - 1 else after, down[c]) for c in range(chunks)
        ]
        return left, right

    here = [read(c, rows) for c in range(chunks)]
    left, right = neighbours(here, zero, zero)
    cross = [(left[c] + right[c]) - 2.0 * here[c] for c in range(chunks)]
    left, right = neighbours(cross, here[0], here[-1])
    result = []
    for c in range(chunks):
        four = CROSS_STIFF * ((left[c] + right[c]) - 2.0 * cross[c])
        along = (read(c, rows - 1) + read(c, rows + 1)) - 2.0 * here[c]
        result.append((stiff[c] * along + (2.0 * TWIST) * cross[c], four))
    return result


def kernel(
    slices, tiles, reach, steps, axles,
    start, stiff_class, packed, class_table, load_table, out,
    w, v, q, four, force, stiff, coarse_stiff, squeeze, spread, prolonged,
    coarse_q, coarse_four, coarse_force, axle, halo,
    a, b, g, e, re, rh,
    axle_send, axle_recv, c0_send, c0_recv, halo_send, halo_recv,
    re_send, re_recv, rh_send, rh_recv,
):
    k, s = lax.axis_index("tm"), lax.axis_index("span")
    prior = lax.rem(k + slices - 1, slices)
    tile, width = start.shape[1], start.shape[2]
    chunks, coarse_chunks = width // 128, width // 512
    coarse_tile = tile // 4
    window = coarse_tile * (2 * reach + 1)
    base = PAD + FAR
    own = PAD + coarse_tile * reach
    deck = tile * tiles
    offsets = list(range(-reach, reach + 1))
    coarse_tau = TIME_STEP * steps
    flat = steps * axles

    def inside(ds):
        return jnp.logical_and(s + ds >= 0, s + ds < tiles)

    def at(ds):
        return pl.ds(own + ds * coarse_tile, coarse_tile)

    barrier = pltpu.get_barrier_semaphore()
    for ds in offsets:
        for kk in range(slices):
            @pl.when(jnp.logical_and(inside(ds), k != kk) if ds == 0 else inside(ds))
            def _(ds=ds, kk=kk):
                pl.semaphore_signal(
                    barrier, inc=1, device_id={"tm": kk, "span": lax.rem(s + ds + tiles, tiles)}, device_id_type=MESH
                )

    for r in range(0, tile, 8):
        for c in range(chunks):
            w[c, base + r:base + r + 8, :] = start[0, r:r + 8, c * 128:(c + 1) * 128]
            v[c, base + r:base + r + 8, :] = start[1, r:r + 8, c * 128:(c + 1) * 128]
    squeeze[...] = jnp.where(
        lax.broadcasted_iota(jnp.int32, (width, width // 4), 0) // 4
        == lax.broadcasted_iota(jnp.int32, (width, width // 4), 1), 1.0 / 16.0, 0.0
    ).astype(jnp.bfloat16)
    spread[...] = jnp.where(
        lax.broadcasted_iota(jnp.int32, (width // 4, width), 1) // 4
        == lax.broadcasted_iota(jnp.int32, (width // 4, width), 0), 1.0, 0.0
    ).astype(jnp.bfloat16)
    classes = stiff_class[...]
    column = jnp.zeros(classes.shape, jnp.float32)
    for i in range(class_table.shape[0]):
        column = jnp.where(classes == i, class_table[i], column)
    for c in range(chunks):
        stiff[c] = jnp.broadcast_to(column[c:c + 1, :], (8, 128))
    wide = jnp.concatenate([stiff[c] for c in range(chunks)], axis=1)
    narrow = 4.0 * split_dot(wide, squeeze[...])
    for c in range(coarse_chunks):
        coarse_stiff[c] = narrow[:, c * 128:(c + 1) * 128]
    axle[k] = packed[...]

    def restricted(first_row, count):
        parts = []
        for field in (w, v):
            parts.append(jnp.concatenate([
                (field[c, pl.ds(first_row, count, stride=4), :]
                 + field[c, pl.ds(first_row + 1, count, stride=4), :])
                + (field[c, pl.ds(first_row + 2, count, stride=4), :]
                   + field[c, pl.ds(first_row + 3, count, stride=4), :])
                for c in range(chunks)
            ], axis=1))
        return split_dot(jnp.concatenate(parts, axis=0), squeeze[...])

    def put(ref, value, first_row, count):
        for f in range(2):
            for c in range(coarse_chunks):
                ref[f, c, first_row:first_row + count, :] = (
                    value[f * count:(f + 1) * count, c * 128:(c + 1) * 128]
                )

    put(a.at[0], restricted(base, coarse_tile), own, coarse_tile)
    for ds in offsets:
        if ds:
            @pl.when(jnp.logical_not(inside(ds)))
            def _(ds=ds):
                a[0, :, :, at(ds), :] = jnp.zeros((2, coarse_chunks, coarse_tile, 128), jnp.float32)

    for place in range(tiles):
        near_tiles = 1 + min(place, reach) + min(tiles - 1 - place, reach)

        @pl.when(s == place)
        def _(near_tiles=near_tiles):
            pl.semaphore_wait(barrier, slices * near_tiles - 1)

    def remote(src, dst, send, recv, kk, ds):
        return pltpu.make_async_remote_copy(
            src_ref=src, dst_ref=dst, send_sem=send, recv_sem=recv,
            device_id={"tm": kk, "span": lax.rem(s + ds + tiles, tiles)}, device_id_type=MESH,
        )

    def axle_copy(kk):
        return remote(axle.at[k], axle.at[k], axle_send.at[kk], axle_recv.at[k], kk, 0)

    def c0_copy(ds):
        return remote(
            a.at[0, :, :, at(0), :], a.at[0, :, :, at(-ds), :],
            c0_send.at[ds + reach], c0_recv.at[reach - ds], k, ds,
        )

    def halo_copy(ds, far):
        side = 0 if ds == 1 else 1
        if ds == 1:
            source, target = (tile - FAR, 0) if far else (tile - NEAR, FAR - NEAR)
        else:
            source, target = (NEAR, NEAR) if far else (0, 0)
        index = 2 * side + far
        return remote(
            start.at[:, pl.ds(source, NEAR), :], halo.at[side, :, pl.ds(target, NEAR), :],
            halo_send.at[index], halo_recv.at[index], k, ds,
        )

    later = [(kk, k < kk) for kk in range(1, slices)]
    for ds in offsets:
        if ds:
            pl.when(inside(ds))(lambda ds=ds: c0_copy(ds).start())
    for kk, wanted in later:
        pl.when(wanted)(lambda kk=kk: axle_copy(kk).start())
    for far in (0, 1):
        for ds in (-1, 1):
            @pl.when(jnp.logical_and(inside(ds), k == 1 if far else k <= 1))
            def _(ds=ds, far=far):
                halo_copy(ds, far).start()

    def slice_axles(j):
        block = axle[j].astype(jnp.float32)
        flipped = jnp.transpose(block[8:16, :])
        kind = flipped[:flat, 2:3]
        weight = jnp.zeros((flat, 1), jnp.float32)
        for i in range(load_table.shape[0]):
            weight = jnp.where(kind == i, load_table[i], weight)
        return block, flipped, weight

    def fine_force(j):
        block, flipped, weight = slice_axles(j)
        terms = [term.astype(jnp.float32) for term in hot_split(TIME_STEP * weight)]
        rows = tile + 2 * FAR
        row = lax.broadcasted_iota(jnp.int32, (rows, 32), 0) + (s * tile - FAR)
        row = row.astype(jnp.float32)
        col = lax.broadcasted_iota(jnp.int32, (axles, width), 1).astype(jnp.float32)
        for t in range(steps):
            row_hot = jnp.where(row == block[t:t + 1, :32], 1.0, 0.0).astype(jnp.bfloat16)
            same = col == flipped[t * axles:(t + 1) * axles, 1:2]
            col_hot = jnp.concatenate(
                [jnp.where(same, term[t * axles:(t + 1) * axles], 0.0) for term in terms]
                + [jnp.zeros((axles, width), jnp.float32)], axis=0
            ).astype(jnp.bfloat16)
            force[t] = jnp.dot(row_hot, col_hot, preferred_element_type=jnp.float32)

    def coarse_forces(j):
        block, flipped, weight = slice_axles(j)
        row = lax.broadcasted_iota(jnp.int32, (window, flat), 0) + (s - reach) * coarse_tile
        row_hot = jnp.where(row.astype(jnp.float32) == block[11:12, :flat], 1.0, 0.0)
        same = (
            lax.broadcasted_iota(jnp.int32, (flat, width // 4), 1).astype(jnp.float32)
            == flipped[:flat, 4:5]
        )
        row_hot = row_hot.astype(jnp.bfloat16)
        total = jnp.zeros((window, width // 4), jnp.float32)
        for term in hot_split(weight * (coarse_tau / (16.0 * steps))):
            col_hot = jnp.where(same, term.astype(jnp.float32), 0.0).astype(jnp.bfloat16)
            total = total + jnp.dot(row_hot, col_hot, preferred_element_type=jnp.float32)
        coarse_force[j] = total

    def on_deck(first_row, value):
        return jnp.where(jnp.logical_and(first_row >= 0, first_row < deck), value, 0.0)

    def coarse_step(state, loads, result):
        for r in range(PAD, PAD + window, 8):
            passed = first_pass(
                lambda c, at_row: state[0, c, pl.ds(at_row, 8), :], r, coarse_chunks,
                [coarse_stiff[c] for c in range(coarse_chunks)],
            )
            for c in range(coarse_chunks):
                coarse_q[c, r:r + 8, :], coarse_four[c, r:r + 8, :] = passed[c]
        for r in range(PAD, PAD + window, 8):
            first = 4 * (r - own) + s * tile
            for c in range(coarse_chunks):
                term = (
                    (coarse_q[c, pl.ds(r - 1, 8), :] + coarse_q[c, pl.ds(r + 1, 8), :])
                    - 2.0 * coarse_q[c, r:r + 8, :] + coarse_four[c, r:r + 8, :]
                )
                speed = (1.0 - coarse_tau * DAMPING) * state[1, c, r:r + 8, :] + (
                    loads[r - PAD:r - PAD + 8, c * 128:(c + 1) * 128]
                    - (coarse_tau / COARSE_SPACING) * term
                )
                result[0, c, r:r + 8, :] = on_deck(
                    first, state[0, c, r:r + 8, :] + coarse_tau * speed
                )
                result[1, c, r:r + 8, :] = on_deck(first, speed)

    def corrected(result, new, fine, old):
        for r in range(PAD, PAD + window, 8):
            first = 4 * (r - own) + s * tile
            rows = slice(r, r + 8)
            for f in range(2):
                for c in range(coarse_chunks):
                    result[f, c, rows, :] = on_deck(
                        first, new[f, c, rows, :] + (fine[f, c, rows, :] - old[f, c, rows, :])
                    )

    def fine_pass(rows):
        passed = first_pass(
            lambda c, at_row: w[c, pl.ds(at_row, 8), :], rows, chunks,
            [stiff[c] for c in range(chunks)],
        )
        for c in range(chunks):
            q[c, rows:rows + 8, :], four[c, rows:rows + 8, :] = passed[c]

    def fine_update(rows, t):
        first = rows - base + s * tile
        for c in range(chunks):
            term = (
                (q[c, pl.ds(rows - 1, 8), :] + q[c, pl.ds(rows + 1, 8), :])
                - 2.0 * q[c, rows:rows + 8, :] + four[c, rows:rows + 8, :]
            )
            speed = (1.0 - TIME_STEP * DAMPING) * v[c, rows:rows + 8, :] + (
                force[t, rows - PAD:rows - PAD + 8, c * 128:(c + 1) * 128] - TIME_STEP * term
            )
            place = w[c, rows:rows + 8, :] + TIME_STEP * speed
            if rows < base or rows >= base + tile:
                speed, place = on_deck(first, speed), on_deck(first, place)
            v[c, rows:rows + 8, :] = speed
            w[c, rows:rows + 8, :] = place

    def sweep(final):
        def up(count):
            return -(-count // 8) * 8

        plan = []
        for t in range(steps):
            need = final + 2 * (steps - 1 - t)
            shape = (up(need), up(need + 1))
            if plan and plan[-1][0] == shape:
                plan[-1][2] = t + 1
            else:
                plan.append([shape, t, t + 1])
        for (rim, rim_q), begin, end in plan:
            def one(t, carry, rim=rim, rim_q=rim_q):
                low, high = base - rim_q, base + tile + rim_q
                for r in range(low, high + 8, 8):
                    if r < high:
                        fine_pass(r)
                    if base - rim <= r - 8 < base + tile + rim:
                        fine_update(r - 8, t)
                return carry

            lax.fori_loop(begin, end, one, 0)

    def prolong_into(value):
        wide = split_dot(value, spread[...])
        for c in range(chunks):
            prolonged[c, :value.shape[0], :] = wide[:, c * 128:(c + 1) * 128]

    upper = lax.broadcasted_iota(jnp.int32, (8, 128), 0) < 4

    def repeated(c, coarse_row):
        return jnp.where(
            upper,
            jnp.broadcast_to(prolonged[c, coarse_row:coarse_row + 1, :], (8, 128)),
            jnp.broadcast_to(prolonged[c, coarse_row + 1:coarse_row + 2, :], (8, 128)),
        )

    def stacked(get):
        return jnp.concatenate(
            [jnp.concatenate([get(f, c) for c in range(coarse_chunks)], axis=1) for f in range(2)],
            axis=0,
        )

    rim_rows = FAR // 4
    side = coarse_tile + 2 * rim_rows
    near_rows = pl.ds(own - rim_rows, side)

    for ds in offsets:
        if ds:
            @pl.when(inside(ds))
            def _(ds=ds):
                remote(
                    a.at[0, :, :, at(0), :], a.at[0, :, :, at(ds), :],
                    c0_send.at[0], c0_recv.at[ds + reach], k, ds,
                ).wait_recv()
    for j in range(slices - 1):
        @pl.when(j < k)
        def _(j=j):
            remote(axle.at[j], axle.at[j], axle_send.at[0], axle_recv.at[j], j, 0).wait_recv()
    for j in range(slices):
        pl.when(j <= k)(lambda j=j: coarse_forces(j))
    coarse_step(a.at[0], coarse_force.at[0], a.at[1])
    for j in range(1, slices - 1):
        pl.when(j < k)(lambda j=j: coarse_step(a.at[j], coarse_force.at[j], a.at[j + 1]))

    @pl.when(k <= 1)
    def _():
        for ds in (-1, 1):
            part = 0 if ds == -1 else 1
            low = PAD if ds == -1 else base + tile

            @pl.when(jnp.logical_not(inside(ds)))
            def _():
                zeros = jnp.zeros((chunks, FAR, 128), jnp.float32)
                w[:, low:low + FAR, :] = zeros
                v[:, low:low + FAR, :] = zeros

            @pl.when(inside(ds))
            def _():
                def landed(far):
                    first_row = NEAR if (ds == -1) != bool(far) else 0
                    index = 2 * part + far
                    return remote(
                        start.at[:, pl.ds(0, NEAR), :], halo.at[part, :, pl.ds(first_row, NEAR), :],
                        halo_send.at[index], halo_recv.at[index], k, ds,
                    )

                landed(0).wait_recv()
                pl.when(k == 1)(lambda: landed(1).wait_recv())
                for c in range(chunks):
                    w[c, low:low + FAR, :] = halo[part, 0, :, c * 128:(c + 1) * 128]
                    v[c, low:low + FAR, :] = halo[part, 1, :, c * 128:(c + 1) * 128]

    @pl.when(k >= 2)
    def _():
        prolong_into(stacked(lambda f, c: a[prior, f, c, near_rows, :]))
        for f, field in enumerate((w, v)):
            for c in range(chunks):
                for i in range(side // 2):
                    field[c, PAD + 8 * i:PAD + 8 * i + 8, :] = repeated(c, f * side + 2 * i)

    def tile_copy(ref, j, send, recv, kk, ds):
        return remote(
            ref.at[j, :, :, at(0), :], ref.at[j, :, :, at(-ds), :],
            send.at[kk, ds + reach], recv.at[j, reach - ds], kk, ds,
        )

    def send_tiles(ref, j, send, recv, wait, skip):
        for kk in range(slices - 1, 0, -1):
            for ds in offsets:
                @pl.when(jnp.logical_and(inside(ds), k + skip < kk))
                def _(kk=kk, ds=ds):
                    copy = tile_copy(ref, j, send, recv, kk, ds)
                    copy.wait_send() if wait else copy.start()

    def receive_tiles(ref, j, send, recv, source):
        for ds in offsets:
            @pl.when(inside(ds))
            def _(ds=ds):
                remote(
                    ref.at[j, :, :, at(0), :], ref.at[j, :, :, at(ds), :],
                    send.at[0, 0], recv.at[j, ds + reach], source, ds,
                ).wait_recv()

    @pl.when(k >= 1)
    def _():
        fine_force(prior)
        sweep(NEAR)
        put(re.at[prior], restricted(PAD, side), own - rim_rows, side)
        pl.when(k >= 2)(lambda: send_tiles(re, prior, re_send, re_recv, False, 0))

    for j in range(slices - 2):
        @pl.when(j + 2 <= k)
        def _(j=j):
            receive_tiles(re, j, re_send, re_recv, j + 1 if j else 0)

    @pl.when(k >= 1)
    def _():
        corrected(b.at[1], a.at[1], re.at[0], a.at[1])
    for j in range(1, slices - 1):
        @pl.when(j < k)
        def _(j=j):
            coarse_step(b.at[j], coarse_force.at[j], g.at[j])
            corrected(b.at[j + 1], g.at[j], re.at[j], a.at[j + 1])

    @pl.when(k >= 1)
    def _():
        prolong_into(stacked(lambda f, c: b[k, f, c, near_rows, :] - re[prior, f, c, near_rows, :]))
        for f, field in enumerate((w, v)):
            for c in range(chunks):
                for i in range(side // 2):
                    rows = slice(PAD + 8 * i, PAD + 8 * i + 8)
                    field[c, rows, :] = field[c, rows, :] + repeated(c, f * side + 2 * i)

    fine_force(k)
    sweep(0)
    mine = restricted(base, coarse_tile)

    @pl.when(k == 0)
    def _():
        put(re.at[0], mine, own, coarse_tile)
        send_tiles(re, 0, re_send, re_recv, False, 1)

    @pl.when(k >= 1)
    def _():
        put(rh.at[k], mine, own, coarse_tile)
        send_tiles(rh, k, rh_send, rh_recv, False, 0)

    @pl.when(k == 0)
    def _():
        corrected(e.at[1], a.at[1], re.at[0], a.at[1])
    for j in range(1, slices):
        @pl.when(j <= k)
        def _(j=j):
            @pl.when(j == k)
            def _():
                coarse_step(b.at[j], coarse_force.at[j], g.at[j])

            if j > 1:
                coarse_step(e.at[j], coarse_force.at[j], e.at[j + 1])
            pl.when(j < k)(lambda: receive_tiles(rh, j, rh_send, rh_recv, j))
            corrected(e.at[j + 1], e.at[j + 1] if j > 1 else g.at[1], rh.at[j], g.at[j])

    prolong_into(stacked(
        lambda f, c: e[k + 1, f, c, at(0), :]
        - mine[f * coarse_tile:(f + 1) * coarse_tile, c * 128:(c + 1) * 128]
    ))
    for f, field in enumerate((w, v)):
        for c in range(chunks):
            for i in range(coarse_tile // 2):
                out[0, f, 8 * i:8 * i + 8, c * 128:(c + 1) * 128] = (
                    field[c, base + 8 * i:base + 8 * i + 8, :]
                    + repeated(c, f * coarse_tile + 2 * i)
                )

    for ds in offsets:
        if ds:
            pl.when(inside(ds))(lambda ds=ds: c0_copy(ds).wait_send())
    for kk, wanted in later:
        pl.when(wanted)(lambda kk=kk: axle_copy(kk).wait_send())
    for far in (0, 1):
        for ds in (-1, 1):
            @pl.when(jnp.logical_and(inside(ds), k == 1 if far else k <= 1))
            def _(ds=ds, far=far):
                halo_copy(ds, far).wait_send()

    @pl.when(k == 0)
    def _():
        send_tiles(re, 0, re_send, re_recv, True, 1)

    @pl.when(k >= 2)
    def _():
        send_tiles(re, prior, re_send, re_recv, True, 0)

    @pl.when(k >= 1)
    def _():
        send_tiles(rh, k, rh_send, rh_recv, True, 0)


def on_device(
    start_state, stiff_class, class_stiffness, axle_rows, axle_cols, axle_class, load_table
):
    slices, tiles = lax.axis_size("tm"), lax.axis_size("span")
    tile, width = start_state.shape[1], start_state.shape[2]
    steps, axles = axle_rows.shape
    flat = steps * axles
    coarse_tile = tile // 4
    reach = min(-(-(2 * slices + 4) // coarse_tile), tiles)
    window = coarse_tile * (2 * reach + 1)
    coarse_rows = window + 2 * PAD
    fine_rows = tile + 2 * FAR + 2 * PAD
    chunks, coarse_chunks = width // 128, width // 512

    per_step = jnp.pad(
        jnp.concatenate([axle_rows] * 3, axis=1), ((0, 0), (0, 128 - 3 * axles)),
        constant_values=-1,
    )
    in_a_row = jnp.stack([
        axle_rows.reshape(flat), axle_cols.reshape(flat), axle_class.reshape(flat),
        axle_rows.reshape(flat) // 4, axle_cols.reshape(flat) // 4,
    ])
    packed = jnp.concatenate([per_step, jnp.pad(in_a_row, ((0, 3), (0, 128 - flat)))], axis=0)

    coarse = (2, coarse_chunks, coarse_rows, 128)
    f32 = jnp.float32
    dma = pltpu.SemaphoreType.DMA
    vmem, smem = pl.BlockSpec(memory_space=pltpu.VMEM), pl.BlockSpec(memory_space=pltpu.SMEM)
    return pl.pallas_call(
        functools.partial(kernel, slices, tiles, reach, steps, axles),
        out_shape=jax.ShapeDtypeStruct((1,) + start_state.shape, f32),
        in_specs=[vmem, vmem, vmem, smem, smem],
        out_specs=vmem,
        scratch_shapes=[
            pltpu.VMEM((chunks, fine_rows, 128), f32),
            pltpu.VMEM((chunks, fine_rows, 128), f32),
            pltpu.VMEM((chunks, fine_rows, 128), f32),
            pltpu.VMEM((chunks, fine_rows, 128), f32),
            pltpu.VMEM((2 * steps, tile + 2 * FAR, width), f32),
            pltpu.VMEM((chunks, 8, 128), f32),
            pltpu.VMEM((coarse_chunks, 8, 128), f32),
            pltpu.VMEM((width, width // 4), jnp.bfloat16),
            pltpu.VMEM((width // 4, width), jnp.bfloat16),
            pltpu.VMEM((chunks, 2 * (coarse_tile + FAR // 2), 128), f32),
            pltpu.VMEM((coarse_chunks, coarse_rows, 128), f32),
            pltpu.VMEM((coarse_chunks, coarse_rows, 128), f32),
            pltpu.VMEM((slices, window, width // 4), f32),
            pltpu.VMEM((slices, 16, 128), jnp.int32),
            pltpu.VMEM((2, 2, FAR, width), f32),
            pltpu.VMEM((slices,) + coarse, f32),
            pltpu.VMEM((slices,) + coarse, f32),
            pltpu.VMEM((slices,) + coarse, f32),
            pltpu.VMEM((slices + 1,) + coarse, f32),
            pltpu.VMEM((slices,) + coarse, f32),
            pltpu.VMEM((slices,) + coarse, f32),
            dma((slices,)), dma((slices,)),
            dma((2 * reach + 1,)), dma((2 * reach + 1,)),
            dma((4,)), dma((4,)),
            dma((slices, 2 * reach + 1)), dma((slices, 2 * reach + 1)),
            dma((slices, 2 * reach + 1)), dma((slices, 2 * reach + 1)),
        ],
        compiler_params=pltpu.CompilerParams(
            collective_id=0, has_side_effects=True, vmem_limit_bytes=52 * 1024 * 1024
        ),
    )(start_state, stiff_class.reshape(chunks, 128), packed, class_stiffness, load_table)


def solution(mesh):
    in_specs = (
        P(None, ("parts", "span"), None),
        P("parts"),
        P(),
        P(("parts", "tm"), None),
        P(("parts", "tm"), None),
        P(("parts", "tm"), None),
        P(),
    )
    out_specs = P("tm", None, ("parts", "span"), None)
    return jax.shard_map(
        on_device, mesh=mesh, in_specs=in_specs, out_specs=out_specs, check_vma=False
    )
```
